32 devices in a mesh: epoch: 16 (over z, x, core), depth: 2 (over y).
Axes of the slice: x: 2, y: 2, z: 4, core: 2. Of those that a mesh axis runs over, the one named last changes fastest.
Arguments:
- slip: bfloat16 [16, 2, 3, 8, 1024], P('epoch', 'depth'), may hold values from -6 to 6
- kernels: float32 [2, 16, 2, 3, 1024], P(None, None, 'depth'), may hold values from -0.07 to 0.07
- lag_index: int32 [16], replicated, may hold values from 0 to 15
- observed: float32 [16, 8, 1024], P('epoch', None, 'depth'), may hold values from -6 to 6
- mask: int32 [16, 8, 1024], P('epoch', None, 'depth'), may hold values 0 or 1
- noise_var: float32 [16], P('epoch'), may hold values from 0.5 to 2
- prior_prec: float32 [2, 3], P('depth'), may hold values from 0.25 to 4
Outputs:
- gradient: float32 [16, 2, 3, 8, 1024], P('epoch', 'depth')
- predicted: float32 [16, 8, 1024], P('epoch', None, 'depth')
The draws below stay inside these ranges and needn't reach their ends.
All inputs are finite; a program needn't handle non-finite values. No bound on the sum of `mask` on one device may be relied on, other than what follows from the above.
Results may differ from the reference program's by a relative error of at most 0.0029.
Values may be sent and summed in bfloat16 or wider, within the bound.
A program may use at most 64 MiB of HBM per device.

```python
import math
import jax
import jax.numpy as jnp
from jax import lax

W = 1024
CHAN = 3
KINDS = 16
ROWS = 8
EPOCHS = 16
LAYERS = 2


def place_ends(array, own_key, low, top_value):
    shape = array.shape
    index_at = [jax.random.randint(jax.random.fold_in(own_key, axis), (), 0, shape[axis]) for axis in range(len(shape))]
    array = array.at[tuple(index_at)].set(low)
    longest = shape.index(max(shape))
    index_at[longest] = (index_at[longest] + 1) % shape[longest]
    return array.at[tuple(index_at)].set(top_value)


def block_scale(stream_key, extent, pieces, least, high):
    factor_of = 1.0
    for dim, blocks in pieces:
        draws = jax.random.uniform(jax.random.fold_in(jax.random.fold_in(stream_key, 6), dim), (blocks,), jnp.float32, least / len(pieces), high / len(pieces))
        factor_of = factor_of * jnp.repeat(jnp.exp(draws), extent[dim] // blocks).reshape((-1,) + (1,) * (len(extent) - 1 - dim))
    return factor_of


def gaussian(stream_key, shape, deviation, limit, pieces=(), held_as=jnp.bfloat16):
    array = jax.random.normal(stream_key, shape, jnp.float32) * deviation
    if len(pieces) > 0:
        array = block_scale(stream_key, shape, pieces, -0.22, 0.18) * array
    return jnp.clip(array, min=-limit, max=limit).astype(held_as)


def setup_inputs(seed: int = 0) -> dict:
    seeds = jax.random.split(jax.random.key(seed), 8)
    return {
        "slip": gaussian(seeds[0], (EPOCHS, LAYERS, CHAN, ROWS, W), 1.0, 6.0, ((0, 16), (1, 2))),
        "kernels": jnp.clip(jax.random.uniform(seeds[1], (2, KINDS, LAYERS, CHAN, W), jnp.float32, -0.07, 0.07) * block_scale(seeds[1], (2, KINDS, LAYERS, CHAN, W), ((2, 2),), -0.4, 0.0), -0.07, 0.07),
        "lag_index": place_ends(jax.random.randint(seeds[2], (EPOCHS,), 0, KINDS), jax.random.fold_in(seeds[2], 1), 0, KINDS - 1).astype(jnp.int32),
        "observed": gaussian(seeds[3], (EPOCHS, ROWS, W), 1.0, 6.0, ((0, 16), (2, 2)), jnp.float32),
        "mask": place_ends((jax.random.randint(seeds[4], (EPOCHS, ROWS, W), 0, 4) < 3).astype(jnp.int32), jax.random.fold_in(seeds[4], 1), 0, 1),
        "noise_var": jnp.clip(jnp.exp(math.log(2.0) - 1.3862944 * jax.random.uniform(seeds[5], (EPOCHS,), jnp.float32) ** block_scale(seeds[5], (EPOCHS,), ((0, 16),), -0.2, 0.2)), 0.5, 2.0),
        "prior_prec": jnp.clip(jnp.exp(math.log(4.0) - 2.7725887 * jax.random.uniform(seeds[6], (LAYERS, CHAN), jnp.float32) ** block_scale(seeds[6], (LAYERS, CHAN), ((0, 2),), -0.2, 0.2)), 0.25, 4.0),
    }


def dft_tables(columns):
    position = lax.iota(jnp.int32, columns)
    product = (position[:, None] * position[None, :]) % columns
    angle = product.astype(jnp.float32) * (2.0 * math.pi / columns)
    cosine = jnp.cos(angle)
    sine = jnp.sin(angle)
    return jnp.concatenate([cosine, -sine], axis=1), jnp.concatenate([cosine, -sine], axis=0)


def lag_weights(lag_values, lag_index, kinds):
    epochs = lag_index.shape[0]
    matches = lag_values[:, None] == lax.iota(jnp.int32, epochs)[None, :]
    kernel_of = jnp.sum(jnp.where(matches, lag_index[None, :], 0), axis=1)
    onehot = (lag_values[:, None] >= 0) & (kernel_of[:, None] == lax.iota(jnp.int32, kinds)[None, :])
    return onehot.astype(jnp.float32)


def reference(slip, kernels, lag_index, observed, mask, noise_var, prior_prec):
    highest = lax.Precision.HIGHEST
    forward_table, inverse_table = dft_tables(W)
    field = slip.astype(jnp.float32).reshape(-1, W)
    spectra = jnp.dot(field, forward_table, precision=highest, preferred_element_type=jnp.float32).astype(jnp.bfloat16)
    spectra = spectra.reshape(EPOCHS, LAYERS, CHAN, ROWS, 2, W)
    spec_re = spectra[:, :, :, :, 0, :].astype(jnp.float32)
    spec_im = spectra[:, :, :, :, 1, :].astype(jnp.float32)
    sources = lax.iota(jnp.int32, EPOCHS)

    def forward_one(target):
        onehot = lag_weights(target - sources, lag_index, KINDS)
        chosen = jnp.einsum("sk,xklcw->xslcw", onehot, kernels, precision=highest)
        real_part = jnp.einsum("slcw,slcrw->rw", chosen[0], spec_re, precision=highest) - jnp.einsum("slcw,slcrw->rw", chosen[1], spec_im, precision=highest)
        imag_part = jnp.einsum("slcw,slcrw->rw", chosen[0], spec_im, precision=highest) + jnp.einsum("slcw,slcrw->rw", chosen[1], spec_re, precision=highest)
        return jnp.concatenate([real_part, imag_part], axis=1)

    pred_spec = lax.map(forward_one, sources)
    predicted = jnp.dot(pred_spec.reshape(-1, 2 * W), inverse_table, precision=highest, preferred_element_type=jnp.float32).reshape(EPOCHS, ROWS, W) / W
    weight = mask.astype(jnp.float32) / noise_var[:, None, None]
    resid = (weight * (predicted - observed)).astype(jnp.bfloat16)
    qspec = jnp.dot(resid.astype(jnp.float32).reshape(-1, W), forward_table, precision=highest, preferred_element_type=jnp.float32).astype(jnp.bfloat16)
    qspec = qspec.reshape(EPOCHS, ROWS, 2, W)
    q_re = qspec[:, :, 0, :].astype(jnp.float32)
    q_im = qspec[:, :, 1, :].astype(jnp.float32)

    def adjoint_one(source):
        onehot = lag_weights(sources - source, lag_index, KINDS)
        chosen = jnp.einsum("tk,xklcw->xtlcw", onehot, kernels, precision=highest)
        real_part = jnp.einsum("tlcw,trw->lcrw", chosen[0], q_re, precision=highest) + jnp.einsum("tlcw,trw->lcrw", chosen[1], q_im, precision=highest)
        imag_part = jnp.einsum("tlcw,trw->lcrw", chosen[0], q_im, precision=highest) - jnp.einsum("tlcw,trw->lcrw", chosen[1], q_re, precision=highest)
        return jnp.concatenate([real_part, imag_part], axis=-1)

    adjoint = lax.map(adjoint_one, sources)
    back = jnp.dot(adjoint.reshape(-1, 2 * W), inverse_table, precision=highest, preferred_element_type=jnp.float32)
    back = back.reshape(EPOCHS, LAYERS, CHAN, ROWS, W) / W
    gradient = -back - prior_prec[None, :, :, None, None] * slip.astype(jnp.float32)
    return gradient, predicted
```

```python
import functools
import math

import jax
import jax.numpy as jnp
import ml_dtypes
import numpy as np
from jax import lax
from jax.experimental import pallas as pl
from jax.experimental.pallas import tpu as pltpu
from jax.sharding import PartitionSpec as P

LANES = 128
PAIR = 2


def tables(columns):
    half = columns // 2
    x = np.arange(columns, dtype=np.int64)
    angle = 2.0 * math.pi * ((x[:, None] * x[None, :half]) % columns) / columns
    low = np.cos(angle)
    high = -np.sin(angle)
    high[:, 0] = 1.0 - 2.0 * (x % 2)
    forward = np.concatenate([low, high], axis=1)
    scale = np.full((columns,), 2.0 / columns)
    scale[0] = scale[half] = 1.0 / columns
    inverse = (forward * scale[None, :]).T

    def split(table):
        table = table.astype(np.float32)
        top = table.astype(ml_dtypes.bfloat16)
        rest = (table - top.astype(np.float32)).astype(ml_dtypes.bfloat16)
        return np.stack([top, rest])

    return split(forward), split(inverse)


def kernel(
    epochs, depths, owners, blocks,
    lag_ref, nv_ref, prior_ref, slip_ref, obs_ref, mask_ref, k_hbm, f_hbm, i_hbm,
    grad_ref, pred_ref,
    f_ref, i_ref, k_ref, send_a, recv_a, send_b, recv_b, send_c, recv_c, send_d, recv_d,
    send_o, recv_o, mirror, kinds_abc, lag_abc, spec, wide,
    load_sem, out_sem, in_sem,
):
    bf16, f32 = jnp.bfloat16, jnp.float32
    channels = slip_ref.shape[2]
    columns = slip_ref.shape[4]
    half = columns // 2
    kinds = k_ref.shape[1]
    width = obs_ref.shape[2]
    pairs = owners // blocks
    total = epochs * depths
    me = lax.axis_index("epoch")
    layer = lax.axis_index("depth")
    flat = me * depths + layer
    everyone_owns = epochs == owners

    load_f = pltpu.make_async_copy(f_hbm, f_ref, load_sem.at[0])
    load_i = pltpu.make_async_copy(i_hbm, i_ref, load_sem.at[1])
    load_k = pltpu.make_async_copy(k_hbm, k_ref, load_sem.at[2])
    load_f.start()
    load_k.start()
    load_i.start()

    barrier = pltpu.get_barrier_semaphore()

    @pl.loop(1, total)
    def _(step):
        other = (flat + step) % total
        pl.semaphore_signal(
            barrier, inc=1, device_id=(other // depths, other % depths),
            device_id_type=pl.DeviceIdType.MESH,
        )

    def remote(src, dst, number, epoch, depth):
        pltpu.make_async_remote_copy(
            src_ref=src, dst_ref=dst, send_sem=out_sem.at[number], recv_sem=in_sem.at[number],
            device_id=(epoch, depth), device_id_type=pl.DeviceIdType.MESH,
        ).start()

    def local(src, dst, number):
        pltpu.make_async_copy(src, dst, in_sem.at[number]).start()

    def wait_bytes(ref, sem):
        pltpu.make_async_copy(ref, ref, sem).wait()

    def to_owners(send, recv, number):
        if everyone_owns:
            @pl.loop(1, owners)
            def _(step):
                owner = (me + step) % owners
                remote(send.at[owner], recv.at[me], number, owner, layer)

            local(send.at[me], recv.at[me], number)
        else:
            @pl.loop(0, owners)
            def _(step):
                owner = (me + step) % owners

                @pl.when(owner != me)
                def _():
                    remote(send.at[owner], recv.at[me], number, owner, layer)

                @pl.when(owner == me)
                def _():
                    local(send.at[me], recv.at[me], number)

    def sent_to_owners(send, number):
        if everyone_owns:
            wait_bytes(send.at[pl.ds(0, owners - 1)], out_sem.at[number])
        else:
            @pl.when(me < owners)
            def _():
                wait_bytes(send.at[pl.ds(0, owners - 1)], out_sem.at[number])

            @pl.when(me >= owners)
            def _():
                wait_bytes(send, out_sem.at[number])

    def owner_part(part):
        if everyone_owns:
            part()
        else:
            pl.when(me < owners)(part)

    def forward(field):
        return jnp.dot(field, f_ref[0], preferred_element_type=f32) + jnp.dot(
            field, f_ref[1], preferred_element_type=f32
        )

    def inverse(value):
        top = value.astype(bf16)
        rest = (value - top.astype(f32)).astype(bf16)
        rows = value.shape[0]
        both = jnp.dot(jnp.concatenate([top, rest]), i_ref[0], preferred_element_type=f32)
        return (both[:rows] + both[rows:]) + jnp.dot(top, i_ref[1], preferred_element_type=f32)

    def scatter(value, send):
        for pair in range(pairs):
            for block in range(blocks):
                rows = slice(pair * 8, pair * 8 + 8)
                real = value[rows, block * LANES : (block + 1) * LANES]
                imag = value[rows, half + block * LANES : half + (block + 1) * LANES]
                send[pair * blocks + block] = jnp.concatenate([real, imag]).astype(bf16)

    send_o[0:8] = obs_ref[0]
    send_o[8:16] = mask_ref[0].astype(f32)

    padded = pairs * 8
    row = lax.broadcasted_iota(jnp.int32, (padded, channels * 8), 0)
    source = lax.broadcasted_iota(jnp.int32, (padded, channels * 8), 1)
    wanted = (row % 8) // PAIR * 8 + row // 8 * PAIR + row % PAIR
    order = ((wanted == source) & (row % 8 < channels * PAIR)).astype(bf16)
    slip_rows = jnp.concatenate([slip_ref[0, 0, c].astype(f32) for c in range(channels)])
    slip_wide = jnp.dot(order, slip_rows.astype(bf16), preferred_element_type=f32)

    load_f.wait()
    scatter(forward(slip_wide.astype(bf16)), send_a)
    pl.semaphore_wait(barrier, total - 1)
    to_owners(send_a, recv_a, 0)

    @pl.loop(1, depths)
    def _(step):
        remote(send_o, recv_o.at[layer], 4, me, (layer + step) % depths)

    local(send_o, recv_o.at[layer], 4)

    load_k.wait()

    def prepare():
        block = me % blocks
        row8 = lax.broadcasted_iota(jnp.int32, (8, LANES), 0)
        lane = lax.broadcasted_iota(jnp.int32, (8, LANES), 1)

        def tile(part, kind, place):
            lanes = pl.ds(pl.multiple_of(place * LANES, LANES), LANES)
            value = k_ref[part, kind, 0, :, lanes]
            out = jnp.zeros((8, LANES), f32)
            for c in range(channels):
                out = jnp.where(row8 // PAIR == c, value[c : c + 1], out)
            return out

        count = 2 * blocks

        @pl.loop(0, kinds)
        def _(kind):
            for part in range(2):
                mirror[part, kind] = tile(part, kind, count - 1 - block)

        j = lax.broadcasted_iota(jnp.int32, (LANES, LANES), 0)
        i = lax.broadcasted_iota(jnp.int32, (LANES, LANES), 1)
        turn = (i + j == LANES).astype(f32)
        turned = jnp.dot(
            mirror[...].reshape(2 * kinds * 8, LANES), turn,
            precision=lax.Precision.HIGHEST, preferred_element_type=f32,
        )
        mirror[...] = turned.reshape(2, kinds, 8, LANES)

        @pl.loop(0, kinds)
        def _(kind):
            first = (count - block) % count
            real = jnp.where(lane == 0, tile(0, kind, first), mirror[0, kind])
            imag = jnp.where(lane == 0, tile(1, kind, first), mirror[1, kind])
            real = 0.5 * (tile(0, kind, block) + real)
            imag = 0.5 * (tile(1, kind, block) - imag)
            middle = tile(0, kind, blocks)
            kinds_abc[kind, 0] = real
            kinds_abc[kind, 1] = imag
            kinds_abc[kind, 2] = jnp.where((lane == 0) & (block == 0), middle, real)

        lag_abc[pl.ds(0, epochs)] = jnp.zeros((epochs, 3, 8, LANES), f32)

        @pl.loop(0, epochs)
        def _(lag):
            lag_abc[epochs + lag] = kinds_abc[lag_ref[lag]]

    owner_part(prepare)

    def unpack(recv):
        @pl.loop(0, epochs)
        def _(epoch):
            value = recv[epoch].astype(f32)
            spec[epoch, 0] = value[0:8]
            spec[epoch, 1] = value[8:16]

    row8 = lax.broadcasted_iota(jnp.int32, (8, LANES), 0)

    def predict():
        wait_bytes(recv_a, in_sem.at[0])
        unpack(recv_a)

        @pl.loop(0, epochs)
        def _(target):
            real = jnp.zeros((8, LANES), f32)
            imag = jnp.zeros((8, LANES), f32)
            for s in range(epochs):
                at = epochs + target - s
                a, b, c = lag_abc[at, 0], lag_abc[at, 1], lag_abc[at, 2]
                sr, si = spec[s, 0], spec[s, 1]
                real = real + (a * sr - b * si)
                imag = imag + (c * si + b * sr)
            real = real + pltpu.roll(real, 4, 0)
            real = real + pltpu.roll(real, 2, 0)
            imag = imag + pltpu.roll(imag, 4, 0)
            imag = imag + pltpu.roll(imag, 2, 0)
            send_b[target] = jnp.where(row8 < 4, real, imag)

        @pl.loop(1, total)
        def _(step):
            other = (flat + step) % total
            epoch = other // depths
            remote(send_b.at[epoch], recv_b.at[layer, me], 1, epoch, other % depths)

        local(send_b.at[me], recv_b.at[layer, me], 1)

    owner_part(predict)

    wait_bytes(recv_o, in_sem.at[4])
    inv = 1.0 / jnp.full((8, columns), nv_ref[0], f32)
    seen = jnp.concatenate([recv_o[d, 0:8] for d in range(depths)], axis=1)
    weight = jnp.concatenate([recv_o[d, 8:16] for d in range(depths)], axis=1) * inv
    rowp = lax.broadcasted_iota(jnp.int32, (padded, 8), 0)
    colp = lax.broadcasted_iota(jnp.int32, (padded, 8), 1)
    spread = (rowp // 8 * PAIR + rowp % PAIR == colp).astype(f32)
    seen_wide = jnp.dot(
        spread, seen, precision=lax.Precision.HIGHEST, preferred_element_type=f32
    )
    weight_wide = jnp.dot(
        spread, weight, precision=lax.Precision.HIGHEST, preferred_element_type=f32
    )
    load_i.wait()

    wait_bytes(recv_b, in_sem.at[1])
    for pair in range(pairs):
        for block in range(blocks):
            value = recv_b[0, pair * blocks + block]
            for d in range(1, depths):
                value = value + recv_b[d, pair * blocks + block]
            turned = pltpu.roll(value, 4, 0)
            rows = slice(pair * 8, pair * 8 + 8)
            wide[rows, block * LANES : (block + 1) * LANES] = jnp.where(row8 < 4, value, turned)
            wide[rows, half + block * LANES : half + (block + 1) * LANES] = jnp.where(
                row8 < 4, turned, value
            )
    predicted = inverse(wide[...])
    resid = (weight_wide * (predicted - seen_wide)).astype(bf16)
    scatter(forward(resid), send_c)
    to_owners(send_c, recv_c, 2)

    wide[...] = predicted
    mine = pl.ds(pl.multiple_of(layer * width, LANES), width)
    for pair in range(pairs):
        pred_ref[0, pair * PAIR : (pair + 1) * PAIR, :] = wide[pair * 8 : pair * 8 + PAIR, mine]

    def adjoint():
        wait_bytes(recv_c, in_sem.at[2])
        unpack(recv_c)

        @pl.loop(0, epochs)
        def _(origin):
            real = jnp.zeros((8, LANES), f32)
            imag = jnp.zeros((8, LANES), f32)
            for t in range(epochs):
                at = epochs + t - origin
                a, b, c = lag_abc[at, 0], lag_abc[at, 1], lag_abc[at, 2]
                qr, qi = spec[t, 0], spec[t, 1]
                real = real + (a * qr + b * qi)
                imag = imag + (c * qi - b * qr)
            send_d[origin, 0:8] = real
            send_d[origin, 8:16] = imag

        @pl.loop(1, epochs)
        def _(step):
            epoch = (me + step) % epochs
            remote(send_d.at[epoch], recv_d.at[me], 3, epoch, layer)

        local(send_d.at[me], recv_d.at[me], 3)

    owner_part(adjoint)

    rowc = lax.broadcasted_iota(jnp.int32, (padded, columns), 0) % 8 // PAIR
    prior = jnp.zeros((padded, columns), f32)
    for c in range(channels):
        prior = jnp.where(rowc == c, prior_ref[0, c], prior)
    prior = prior * slip_wide

    wait_bytes(recv_d, in_sem.at[3])
    for pair in range(pairs):
        for block in range(blocks):
            rows = slice(pair * 8, pair * 8 + 8)
            wide[rows, block * LANES : (block + 1) * LANES] = recv_d[pair * blocks + block, 0:8]
            wide[rows, half + block * LANES : half + (block + 1) * LANES] = recv_d[
                pair * blocks + block, 8:16
            ]
    result = -inverse(wide[...]) - prior
    for pair in range(pairs):
        for c in range(channels):
            first = pair * 8 + c * PAIR
            grad_ref[0, 0, c, pair * PAIR : (pair + 1) * PAIR, :] = result[first : first + PAIR]

    sent_to_owners(send_a, 0)
    sent_to_owners(send_c, 2)

    def sent():
        @pl.loop(1, total)
        def _(step):
            wait_bytes(send_b.at[0], out_sem.at[1])

        wait_bytes(send_d.at[pl.ds(0, epochs - 1)], out_sem.at[3])

    owner_part(sent)

    @pl.loop(1, depths)
    def _(step):
        wait_bytes(send_o, out_sem.at[4])


def body(epochs, depths, slip, kernels, lag_index, observed, mask, noise_var, prior_prec):
    columns = slip.shape[-1]
    channels = slip.shape[2]
    kinds = kernels.shape[1]
    rows = slip.shape[3]
    blocks = columns // 2 // LANES
    owners = blocks * rows // PAIR
    padded = rows // PAIR * 8
    forward_table, inverse_table = tables(columns)
    f32, bf16 = jnp.float32, jnp.bfloat16
    vmem = pl.BlockSpec(memory_space=pltpu.VMEM)
    smem = pl.BlockSpec(memory_space=pltpu.SMEM)
    hbm = pl.BlockSpec(memory_space=pl.ANY)
    return pl.pallas_call(
        functools.partial(kernel, epochs, depths, owners, blocks),
        out_shape=(
            jax.ShapeDtypeStruct(slip.shape, f32),
            jax.ShapeDtypeStruct(observed.shape, f32),
        ),
        in_specs=[smem, smem, smem, vmem, vmem, vmem, hbm, hbm, hbm],
        out_specs=(vmem, vmem),
        scratch_shapes=[
            pltpu.VMEM((2, columns, columns), bf16),
            pltpu.VMEM((2, columns, columns), bf16),
            pltpu.VMEM(kernels.shape, f32),
            pltpu.VMEM((owners, 16, LANES), bf16),
            pltpu.VMEM((epochs, 16, LANES), bf16),
            pltpu.VMEM((epochs, 8, LANES), f32),
            pltpu.VMEM((depths, owners, 8, LANES), f32),
            pltpu.VMEM((owners, 16, LANES), bf16),
            pltpu.VMEM((epochs, 16, LANES), bf16),
            pltpu.VMEM((epochs, 16, LANES), f32),
            pltpu.VMEM((owners, 16, LANES), f32),
            pltpu.VMEM((16, observed.shape[2]), f32),
            pltpu.VMEM((depths, 16, observed.shape[2]), f32),
            pltpu.VMEM((2, kinds, 8, LANES), f32),
            pltpu.VMEM((kinds, 3, 8, LANES), f32),
            pltpu.VMEM((2 * epochs, 3, 8, LANES), f32),
            pltpu.VMEM((epochs, 2, 8, LANES), f32),
            pltpu.VMEM((padded, columns), f32),
            pltpu.SemaphoreType.DMA((3,)),
            pltpu.SemaphoreType.DMA((5,)),
            pltpu.SemaphoreType.DMA((5,)),
        ],
        compiler_params=pltpu.CompilerParams(
            collective_id=0, has_side_effects=True, vmem_limit_bytes=40 * 1024 * 1024
        ),
    )(
        lag_index, noise_var, prior_prec, slip, observed, mask, kernels,
        jnp.asarray(forward_table), jnp.asarray(inverse_table),
    )


def solution(mesh):
    in_specs = (
        P("epoch", "depth", None, None, None),
        P(None, None, "depth", None, None),
        P(),
        P("epoch", None, "depth"),
        P("epoch", None, "depth"),
        P("epoch"),
        P("depth", None),
    )
    out_specs = (P("epoch", "depth", None, None, None), P("epoch", None, "depth"))
    run = functools.partial(body, mesh.shape["epoch"], mesh.shape["depth"])
    return jax.shard_map(run, mesh=mesh, in_specs=in_specs, out_specs=out_specs, check_vma=False)
```

```python
import functools
import math

import jax
import jax.numpy as jnp
import ml_dtypes
import numpy as np
from jax import lax
from jax.experimental import pallas as pl
from jax.experimental.pallas import tpu as pltpu
from jax.sharding import PartitionSpec as P

LANES = 128
PAIR = 2


def tables(columns):
    half = columns // 2
    x = np.arange(columns, dtype=np.int64)
    angle = 2.0 * math.pi * ((x[:, None] * x[None, :half]) % columns) / columns
    low = np.cos(angle)
    high = -np.sin(angle)
    high[:, 0] = 1.0 - 2.0 * (x % 2)
    forward = np.concatenate([low, high], axis=1)
    scale = np.full((columns,), 2.0 / columns)
    scale[0] = scale[half] = 1.0 / columns
    inverse = (forward * scale[None, :]).T

    def split(table):
        table = table.astype(np.float32)
        top = table.astype(ml_dtypes.bfloat16)
        rest = (table - top.astype(np.float32)).astype(ml_dtypes.bfloat16)
        return np.stack([top, rest])

    return split(forward), split(inverse)


def kernel(
    epochs, depths, owners, blocks,
    lag_ref, nv_ref, prior_ref, slip_hbm, obs_hbm, mask_hbm, k_hbm, f_hbm, i_hbm,
    grad_ref, pred_ref,
    slip_ref, obs_ref, mask_ref, f_ref, i_ref, k_ref, send_a, recv_a, send_b, recv_b, send_c, recv_c, send_d, recv_d,
    send_o, recv_o, mirror, kinds_abc, lag_abc, spec, wide,
    load_sem, out_sem, in_sem,
):
    bf16, f32 = jnp.bfloat16, jnp.float32
    channels = slip_ref.shape[2]
    columns = slip_ref.shape[4]
    half = columns // 2
    kinds = k_ref.shape[1]
    width = obs_ref.shape[2]
    pairs = owners // blocks
    total = epochs * depths
    me = lax.axis_index("epoch")
    layer = lax.axis_index("depth")
    flat = me * depths + layer
    everyone_owns = epochs == owners

    load_f = pltpu.make_async_copy(f_hbm, f_ref, load_sem.at[0])
    load_i = pltpu.make_async_copy(i_hbm, i_ref, load_sem.at[1])
    load_k = pltpu.make_async_copy(k_hbm, k_ref, load_sem.at[2])
    load_s = pltpu.make_async_copy(slip_hbm, slip_ref, load_sem.at[3])
    load_o = pltpu.make_async_copy(obs_hbm, obs_ref, load_sem.at[4])
    load_m = pltpu.make_async_copy(mask_hbm, mask_ref, load_sem.at[5])
    load_k.start()
    load_s.start()
    load_o.start()
    load_m.start()
    load_f.start()
    load_i.start()

    barrier = pltpu.get_barrier_semaphore()

    @pl.loop(1, total)
    def _(step):
        other = (flat + step) % total
        pl.semaphore_signal(
            barrier, inc=1, device_id=(other // depths, other % depths),
            device_id_type=pl.DeviceIdType.MESH,
        )

    def remote(src, dst, number, epoch, depth):
        pltpu.make_async_remote_copy(
            src_ref=src, dst_ref=dst, send_sem=out_sem.at[number], recv_sem=in_sem.at[number],
            device_id=(epoch, depth), device_id_type=pl.DeviceIdType.MESH,
        ).start()

    def local(src, dst, number):
        pltpu.make_async_copy(src, dst, in_sem.at[number]).start()

    def wait_bytes(ref, sem):
        pltpu.make_async_copy(ref, ref, sem).wait()

    def to_owners(send, recv, number):
        if everyone_owns:
            @pl.loop(1, owners)
            def _(step):
                owner = (me + step) % owners
                remote(send.at[owner], recv.at[me], number, owner, layer)

            local(send.at[me], recv.at[me], number)
        else:
            @pl.loop(0, owners)
            def _(step):
                owner = (me + step) % owners

                @pl.when(owner != me)
                def _():
                    remote(send.at[owner], recv.at[me], number, owner, layer)

                @pl.when(owner == me)
                def _():
                    local(send.at[me], recv.at[me], number)

    def sent_to_owners(send, number):
        if everyone_owns:
            wait_bytes(send.at[pl.ds(0, owners - 1)], out_sem.at[number])
        else:
            @pl.when(me < owners)
            def _():
                wait_bytes(send.at[pl.ds(0, owners - 1)], out_sem.at[number])

            @pl.when(me >= owners)
            def _():
                wait_bytes(send, out_sem.at[number])

    def owner_part(part):
        if everyone_owns:
            part()
        else:
            pl.when(me < owners)(part)

    def forward(field):
        return jnp.dot(field, f_ref[0], preferred_element_type=f32) + jnp.dot(
            field, f_ref[1], preferred_element_type=f32
        )

    def inverse(value):
        top = value.astype(bf16)
        rest = (value - top.astype(f32)).astype(bf16)
        rows = value.shape[0]
        both = jnp.dot(jnp.concatenate([top, rest]), i_ref[0], preferred_element_type=f32)
        return (both[:rows] + both[rows:]) + jnp.dot(top, i_ref[1], preferred_element_type=f32)

    def scatter(value, send):
        for pair in range(pairs):
            for block in range(blocks):
                rows = slice(pair * 8, pair * 8 + 8)
                real = value[rows, block * LANES : (block + 1) * LANES]
                imag = value[rows, half + block * LANES : half + (block + 1) * LANES]
                send[pair * blocks + block] = jnp.concatenate([real, imag]).astype(bf16)

    load_k.wait()

    def prepare():
        block = me % blocks
        row8 = lax.broadcasted_iota(jnp.int32, (8, LANES), 0)
        lane = lax.broadcasted_iota(jnp.int32, (8, LANES), 1)

        def tile(part, kind, place):
            lanes = pl.ds(pl.multiple_of(place * LANES, LANES), LANES)
            out = jnp.zeros((8, LANES), f32)
            for c in range(channels):
                out = jnp.where(row8 // PAIR == c, k_ref[part, kind, c, :, lanes], out)
            return out

        count = 2 * blocks

        @pl.loop(0, kinds)
        def _(kind):
            for part in range(2):
                mirror[part, kind] = tile(part, kind, count - 1 - block)

        j = lax.broadcasted_iota(jnp.int32, (LANES, LANES), 0)
        i = lax.broadcasted_iota(jnp.int32, (LANES, LANES), 1)
        turn = (i + j == LANES).astype(f32)
        turned = jnp.dot(
            mirror[...].reshape(2 * kinds * 8, LANES), turn,
            precision=lax.Precision.HIGHEST, preferred_element_type=f32,
        )
        mirror[...] = turned.reshape(2, kinds, 8, LANES)

        @pl.loop(0, kinds)
        def _(kind):
            first = (count - block) % count
            real = jnp.where(lane == 0, tile(0, kind, first), mirror[0, kind])
            imag = jnp.where(lane == 0, tile(1, kind, first), mirror[1, kind])
            real = 0.5 * (tile(0, kind, block) + real)
            imag = 0.5 * (tile(1, kind, block) - imag)
            middle = tile(0, kind, blocks)
            kinds_abc[kind, 0] = real
            kinds_abc[kind, 1] = imag
            kinds_abc[kind, 2] = jnp.where((lane == 0) & (block == 0), middle, real)

        lag_abc[pl.ds(0, epochs)] = jnp.zeros((epochs, 3, 8, LANES), f32)

        @pl.loop(0, epochs)
        def _(lag):
            lag_abc[epochs + lag] = kinds_abc[lag_ref[lag]]

    owner_part(prepare)

    load_o.wait()
    load_m.wait()
    send_o[0:8] = obs_ref[0]
    send_o[8:16] = mask_ref[0].astype(f32)

    padded = pairs * 8
    row = lax.broadcasted_iota(jnp.int32, (padded, channels * 8), 0)
    source = lax.broadcasted_iota(jnp.int32, (padded, channels * 8), 1)
    wanted = (row % 8) // PAIR * 8 + row // 8 * PAIR + row % PAIR
    order = ((wanted == source) & (row % 8 < channels * PAIR)).astype(bf16)
    load_s.wait()
    slip_rows = jnp.concatenate([slip_ref[0, 0, c].astype(f32) for c in range(channels)])
    slip_wide = jnp.dot(order, slip_rows.astype(bf16), preferred_element_type=f32)

    load_f.wait()
    scatter(forward(slip_wide.astype(bf16)), send_a)
    pl.semaphore_wait(barrier, total - 1)
    to_owners(send_a, recv_a, 0)

    @pl.loop(1, depths)
    def _(step):
        remote(send_o, recv_o.at[layer], 4, me, (layer + step) % depths)

    local(send_o, recv_o.at[layer], 4)

    def unpack(recv):
        @pl.loop(0, epochs)
        def _(epoch):
            value = recv[epoch].astype(f32)
            spec[epoch, 0] = value[0:8]
            spec[epoch, 1] = value[8:16]

    row8 = lax.broadcasted_iota(jnp.int32, (8, LANES), 0)

    def predict():
        wait_bytes(recv_a, in_sem.at[0])
        unpack(recv_a)

        @pl.loop(1, epochs + 1)
        def _(step):
            target = (me + step) % epochs
            real = jnp.zeros((8, LANES), f32)
            imag = jnp.zeros((8, LANES), f32)
            for s in range(epochs):
                at = epochs + target - s
                a, b, c = lag_abc[at, 0], lag_abc[at, 1], lag_abc[at, 2]
                sr, si = spec[s, 0], spec[s, 1]
                real = real + (a * sr - b * si)
                imag = imag + (c * si + b * sr)
            real = real + pltpu.roll(real, 4, 0)
            real = real + pltpu.roll(real, 2, 0)
            imag = imag + pltpu.roll(imag, 4, 0)
            imag = imag + pltpu.roll(imag, 2, 0)
            send_b[target] = jnp.where(row8 < 4, real, imag)

            for turn in range(1, depths):
                remote(send_b.at[target], recv_b.at[layer, me], 1, target, (layer + turn) % depths)

            @pl.when(step < epochs)
            def _():
                remote(send_b.at[target], recv_b.at[layer, me], 1, target, layer)

        local(send_b.at[me], recv_b.at[layer, me], 1)

    owner_part(predict)

    wait_bytes(recv_o, in_sem.at[4])
    inv = 1.0 / jnp.full((8, columns), nv_ref[0], f32)
    seen = jnp.concatenate([recv_o[d, 0:8] for d in range(depths)], axis=1)
    weight = jnp.concatenate([recv_o[d, 8:16] for d in range(depths)], axis=1) * inv
    rowp = lax.broadcasted_iota(jnp.int32, (padded, 8), 0)
    colp = lax.broadcasted_iota(jnp.int32, (padded, 8), 1)
    spread = (rowp // 8 * PAIR + rowp % PAIR == colp).astype(f32)
    seen_wide = jnp.dot(
        spread, seen, precision=lax.Precision.HIGHEST, preferred_element_type=f32
    )
    weight_wide = jnp.dot(
        spread, weight, precision=lax.Precision.HIGHEST, preferred_element_type=f32
    )
    load_i.wait()

    wait_bytes(recv_b, in_sem.at[1])
    for pair in range(pairs):
        for block in range(blocks):
            value = recv_b[0, pair * blocks + block]
            for d in range(1, depths):
                value = value + recv_b[d, pair * blocks + block]
            turned = pltpu.roll(value, 4, 0)
            rows = slice(pair * 8, pair * 8 + 8)
            wide[rows, block * LANES : (block + 1) * LANES] = jnp.where(row8 < 4, value, turned)
            wide[rows, half + block * LANES : half + (block + 1) * LANES] = jnp.where(
                row8 < 4, turned, value
            )
    predicted = inverse(wide[...])
    resid = (weight_wide * (predicted - seen_wide)).astype(bf16)
    scatter(forward(resid), send_c)
    to_owners(send_c, recv_c, 2)

    wide[...] = predicted
    mine = pl.ds(pl.multiple_of(layer * width, LANES), width)
    for pair in range(pairs):
        pred_ref[0, pair * PAIR : (pair + 1) * PAIR, :] = wide[pair * 8 : pair * 8 + PAIR, mine]

    def adjoint():
        wait_bytes(recv_c, in_sem.at[2])
        unpack(recv_c)

        @pl.loop(1, epochs + 1)
        def _(step):
            origin = (me + step) % epochs
            real = jnp.zeros((8, LANES), f32)
            imag = jnp.zeros((8, LANES), f32)
            for t in range(epochs):
                at = epochs + t - origin
                a, b, c = lag_abc[at, 0], lag_abc[at, 1], lag_abc[at, 2]
                qr, qi = spec[t, 0], spec[t, 1]
                real = real + (a * qr + b * qi)
                imag = imag + (c * qi - b * qr)
            send_d[origin, 0:8] = real
            send_d[origin, 8:16] = imag

            @pl.when(step < epochs)
            def _():
                remote(send_d.at[origin], recv_d.at[me], 3, origin, layer)

        local(send_d.at[me], recv_d.at[me], 3)

    owner_part(adjoint)

    rowc = lax.broadcasted_iota(jnp.int32, (padded, columns), 0) % 8 // PAIR
    prior = jnp.zeros((padded, columns), f32)
    for c in range(channels):
        prior = jnp.where(rowc == c, prior_ref[0, c], prior)
    prior = prior * slip_wide

    wait_bytes(recv_d, in_sem.at[3])
    for pair in range(pairs):
        for block in range(blocks):
            rows = slice(pair * 8, pair * 8 + 8)
            wide[rows, block * LANES : (block + 1) * LANES] = recv_d[pair * blocks + block, 0:8]
            wide[rows, half + block * LANES : half + (block + 1) * LANES] = recv_d[
                pair * blocks + block, 8:16
            ]
    result = -inverse(wide[...]) - prior
    for pair in range(pairs):
        for c in range(channels):
            first = pair * 8 + c * PAIR
            grad_ref[0, 0, c, pair * PAIR : (pair + 1) * PAIR, :] = result[first : first + PAIR]

    sent_to_owners(send_a, 0)
    sent_to_owners(send_c, 2)

    def sent():
        @pl.loop(1, total)
        def _(step):
            wait_bytes(send_b.at[0], out_sem.at[1])

        wait_bytes(send_d.at[pl.ds(0, epochs - 1)], out_sem.at[3])

    owner_part(sent)

    @pl.loop(1, depths)
    def _(step):
        wait_bytes(send_o, out_sem.at[4])


def body(epochs, depths, slip, kernels, lag_index, observed, mask, noise_var, prior_prec):
    columns = slip.shape[-1]
    channels = slip.shape[2]
    kinds = kernels.shape[1]
    rows = slip.shape[3]
    blocks = columns // 2 // LANES
    owners = blocks * rows // PAIR
    padded = rows // PAIR * 8
    forward_table, inverse_table = tables(columns)
    f32, bf16 = jnp.float32, jnp.bfloat16
    vmem = pl.BlockSpec(memory_space=pltpu.VMEM)
    smem = pl.BlockSpec(memory_space=pltpu.SMEM)
    hbm = pl.BlockSpec(memory_space=pltpu.HBM)
    kernels = jnp.swapaxes(kernels, 2, 3)
    return pl.pallas_call(
        functools.partial(kernel, epochs, depths, owners, blocks),
        out_shape=(
            jax.ShapeDtypeStruct(slip.shape, f32),
            jax.ShapeDtypeStruct(observed.shape, f32),
        ),
        in_specs=[smem, smem, smem, hbm, hbm, hbm, hbm, hbm, hbm],
        out_specs=(vmem, vmem),
        scratch_shapes=[
            pltpu.VMEM(slip.shape, bf16),
            pltpu.VMEM(observed.shape, f32),
            pltpu.VMEM(mask.shape, mask.dtype),
            pltpu.VMEM((2, columns, columns), bf16),
            pltpu.VMEM((2, columns, columns), bf16),
            pltpu.VMEM(kernels.shape, f32),
            pltpu.VMEM((owners, 16, LANES), bf16),
            pltpu.VMEM((epochs, 16, LANES), bf16),
            pltpu.VMEM((epochs, 8, LANES), f32),
            pltpu.VMEM((depths, owners, 8, LANES), f32),
            pltpu.VMEM((owners, 16, LANES), bf16),
            pltpu.VMEM((epochs, 16, LANES), bf16),
            pltpu.VMEM((epochs, 16, LANES), f32),
            pltpu.VMEM((owners, 16, LANES), f32),
            pltpu.VMEM((16, observed.shape[2]), f32),
            pltpu.VMEM((depths, 16, observed.shape[2]), f32),
            pltpu.VMEM((2, kinds, 8, LANES), f32),
            pltpu.VMEM((kinds, 3, 8, LANES), f32),
            pltpu.VMEM((2 * epochs, 3, 8, LANES), f32),
            pltpu.VMEM((epochs, 2, 8, LANES), f32),
            pltpu.VMEM((padded, columns), f32),
            pltpu.SemaphoreType.DMA((6,)),
            pltpu.SemaphoreType.DMA((5,)),
            pltpu.SemaphoreType.DMA((5,)),
        ],
        compiler_params=pltpu.CompilerParams(
            collective_id=0, has_side_effects=True, vmem_limit_bytes=60 * 1024 * 1024
        ),
    )(
        lag_index, noise_var, prior_prec, slip, observed, mask, kernels,
        jnp.asarray(forward_table), jnp.asarray(inverse_table),
    )


def solution(mesh):
    in_specs = (
        P("epoch", "depth", None, None, None),
        P(None, None, "depth", None, None),
        P(),
        P("epoch", None, "depth"),
        P("epoch", None, "depth"),
        P("epoch"),
        P("depth", None),
    )
    out_specs = (P("epoch", "depth", None, None, None), P("epoch", None, "depth"))
    run = functools.partial(body, mesh.shape["epoch"], mesh.shape["depth"])
    return jax.shard_map(run, mesh=mesh, in_specs=in_specs, out_specs=out_specs, check_vma=False)
```

```python
import functools
import math

import jax
import jax.numpy as jnp
import ml_dtypes
import numpy as np
from jax import lax
from jax.experimental import pallas as pl
from jax.experimental.pallas import tpu as pltpu
from jax.sharding import PartitionSpec as P

LANES = 128
PAIR = 2


def tables(columns):
    half = columns // 2
    x = np.arange(columns, dtype=np.int64)
    angle = 2.0 * math.pi * ((x[:, None] * x[None, :half]) % columns) / columns
    low = np.cos(angle)
    high = -np.sin(angle)
    high[:, 0] = 1.0 - 2.0 * (x % 2)
    forward = np.concatenate([low, high], axis=1)
    scale = np.full((columns,), 2.0 / columns)
    scale[0] = scale[half] = 1.0 / columns
    inverse = (forward * scale[None, :]).T

    def split(table):
        table = table.astype(np.float32)
        top = table.astype(ml_dtypes.bfloat16)
        rest = (table - top.astype(np.float32)).astype(ml_dtypes.bfloat16)
        return np.stack([top, rest])

    return split(forward), split(inverse)


def kernel(
    epochs, depths, owners, blocks,
    lag_ref, nv_ref, prior_ref, slip_hbm, obs_hbm, mask_hbm, k_hbm, f_hbm, i_hbm,
    grad_ref, pred_ref,
    slip_ref, obs_ref, mask_ref, f_ref, i_ref, k_ref, send_a, recv_a, send_b, recv_b, send_c, recv_c, send_d, recv_d,
    send_o, recv_o, mirror, kinds_abc, lag_abc, spec, wide,
    load_sem, out_sem, in_sem,
):
    bf16, f32 = jnp.bfloat16, jnp.float32
    channels = slip_ref.shape[2]
    columns = slip_ref.shape[4]
    half = columns // 2
    kinds = k_ref.shape[1]
    width = obs_ref.shape[2]
    pairs = owners // blocks
    total = epochs * depths
    me = lax.axis_index("epoch")
    layer = lax.axis_index("depth")
    flat = me * depths + layer
    everyone_owns = epochs == owners

    load_f = pltpu.make_async_copy(f_hbm, f_ref, load_sem.at[0])
    load_i = pltpu.make_async_copy(i_hbm, i_ref, load_sem.at[1])
    load_k = pltpu.make_async_copy(k_hbm, k_ref, load_sem.at[2])
    load_s = pltpu.make_async_copy(slip_hbm, slip_ref, load_sem.at[3])
    load_o = pltpu.make_async_copy(obs_hbm, obs_ref, load_sem.at[4])
    load_m = pltpu.make_async_copy(mask_hbm, mask_ref, load_sem.at[5])
    load_k.start()
    load_s.start()
    load_o.start()
    load_m.start()
    load_f.start()
    load_i.start()

    barrier = pltpu.get_barrier_semaphore()

    @pl.loop(1, total)
    def _(step):
        other = (flat + step) % total
        pl.semaphore_signal(
            barrier, inc=1, device_id=(other // depths, other % depths),
            device_id_type=pl.DeviceIdType.MESH,
        )

    def remote(src, dst, number, epoch, depth):
        pltpu.make_async_remote_copy(
            src_ref=src, dst_ref=dst, send_sem=out_sem.at[number], recv_sem=in_sem.at[number],
            device_id=(epoch, depth), device_id_type=pl.DeviceIdType.MESH,
        ).start()

    def local(src, dst, number):
        pltpu.make_async_copy(src, dst, in_sem.at[number]).start()

    def wait_bytes(ref, sem):
        pltpu.make_async_copy(ref, ref, sem).wait()

    def to_owners(send, recv, number):
        if everyone_owns:
            @pl.loop(1, owners)
            def _(step):
                owner = (me + step) % owners
                remote(send.at[owner], recv.at[me], number, owner, layer)

            local(send.at[me], recv.at[me], number)
        else:
            @pl.loop(0, owners)
            def _(step):
                owner = (me + step) % owners

                @pl.when(owner != me)
                def _():
                    remote(send.at[owner], recv.at[me], number, owner, layer)

                @pl.when(owner == me)
                def _():
                    local(send.at[me], recv.at[me], number)

    def sent_to_owners(send, number):
        if everyone_owns:
            wait_bytes(send.at[pl.ds(0, owners - 1)], out_sem.at[number])
        else:
            @pl.when(me < owners)
            def _():
                wait_bytes(send.at[pl.ds(0, owners - 1)], out_sem.at[number])

            @pl.when(me >= owners)
            def _():
                wait_bytes(send, out_sem.at[number])

    def owner_part(part):
        if everyone_owns:
            part()
        else:
            pl.when(me < owners)(part)

    def forward(field):
        return jnp.dot(field, f_ref[0], preferred_element_type=f32) + jnp.dot(
            field, f_ref[1], preferred_element_type=f32
        )

    def inverse(value):
        top = value.astype(bf16)
        rest = (value - top.astype(f32)).astype(bf16)
        rows = value.shape[0]
        both = jnp.dot(jnp.concatenate([top, rest]), i_ref[0], preferred_element_type=f32)
        return (both[:rows] + both[rows:]) + jnp.dot(top, i_ref[1], preferred_element_type=f32)

    def scatter(value, send):
        for pair in range(pairs):
            for block in range(blocks):
                rows = slice(pair * 8, pair * 8 + 8)
                real = value[rows, block * LANES : (block + 1) * LANES]
                imag = value[rows, half + block * LANES : half + (block + 1) * LANES]
                send[pair * blocks + block] = jnp.concatenate([real, imag]).astype(bf16)

    load_k.wait()

    def prepare():
        block = me % blocks
        row8 = lax.broadcasted_iota(jnp.int32, (8, LANES), 0)
        lane = lax.broadcasted_iota(jnp.int32, (8, LANES), 1)

        def tile(part, kind, place):
            lanes = pl.ds(pl.multiple_of(place * LANES, LANES), LANES)
            out = jnp.zeros((8, LANES), f32)
            for c in range(channels):
                out = jnp.where(row8 // PAIR == c, k_ref[part, kind, c, :, lanes], out)
            return out

        count = 2 * blocks

        @pl.loop(0, kinds)
        def _(kind):
            for part in range(2):
                mirror[part, kind] = tile(part, kind, count - 1 - block)

        j = lax.broadcasted_iota(jnp.int32, (LANES, LANES), 0)
        i = lax.broadcasted_iota(jnp.int32, (LANES, LANES), 1)
        turn = (i + j == LANES).astype(f32)
        turned = jnp.dot(
            mirror[...].reshape(2 * kinds * 8, LANES), turn,
            precision=lax.Precision.HIGHEST, preferred_element_type=f32,
        )
        mirror[...] = turned.reshape(2, kinds, 8, LANES)

        @pl.loop(0, kinds)
        def _(kind):
            first = (count - block) % count
            real = jnp.where(lane == 0, tile(0, kind, first), mirror[0, kind])
            imag = jnp.where(lane == 0, tile(1, kind, first), mirror[1, kind])
            real = 0.5 * (tile(0, kind, block) + real)
            imag = 0.5 * (tile(1, kind, block) - imag)
            middle = tile(0, kind, blocks)
            kinds_abc[kind, 0] = real
            kinds_abc[kind, 1] = imag
            kinds_abc[kind, 2] = jnp.where((lane == 0) & (block == 0), middle, real)

        lag_abc[pl.ds(0, epochs)] = jnp.zeros((epochs, 3, 8, LANES), f32)

        @pl.loop(0, epochs)
        def _(lag):
            lag_abc[epochs + lag] = kinds_abc[lag_ref[lag]]

    owner_part(prepare)

    load_o.wait()
    load_m.wait()
    send_o[0:8] = obs_ref[0]
    send_o[8:16] = mask_ref[0].astype(f32)

    padded = pairs * 8
    row = lax.broadcasted_iota(jnp.int32, (padded, channels * 8), 0)
    source = lax.broadcasted_iota(jnp.int32, (padded, channels * 8), 1)
    wanted = (row % 8) // PAIR * 8 + row // 8 * PAIR + row % PAIR
    order = ((wanted == source) & (row % 8 < channels * PAIR)).astype(bf16)
    load_s.wait()
    slip_rows = jnp.concatenate([slip_ref[0, 0, c].astype(f32) for c in range(channels)])
    slip_wide = jnp.dot(order, slip_rows.astype(bf16), preferred_element_type=f32)

    load_f.wait()
    scatter(forward(slip_wide.astype(bf16)), send_a)
    pl.semaphore_wait(barrier, total - 1)
    to_owners(send_a, recv_a, 0)

    @pl.loop(1, depths)
    def _(step):
        remote(send_o, recv_o.at[layer], 4, me, (layer + step) % depths)

    local(send_o, recv_o.at[layer], 4)

    def unpack(recv):
        @pl.loop(0, epochs)
        def _(epoch):
            value = recv[epoch].astype(f32)
            spec[epoch, 0] = value[0:8]
            spec[epoch, 1] = value[8:16]

    row8 = lax.broadcasted_iota(jnp.int32, (8, LANES), 0)

    def predict():
        wait_bytes(recv_a, in_sem.at[0])
        unpack(recv_a)

        @pl.loop(1, epochs + 1)
        def _(step):
            target = (me + step) % epochs
            real = jnp.zeros((8, LANES), f32)
            imag = jnp.zeros((8, LANES), f32)
            for s in range(epochs):
                at = epochs + target - s
                a, b, c = lag_abc[at, 0], lag_abc[at, 1], lag_abc[at, 2]
                sr, si = spec[s, 0], spec[s, 1]
                real = real + (a * sr - b * si)
                imag = imag + (c * si + b * sr)
            real = real + pltpu.roll(real, 4, 0)
            real = real + pltpu.roll(real, 2, 0)
            imag = imag + pltpu.roll(imag, 4, 0)
            imag = imag + pltpu.roll(imag, 2, 0)
            send_b[target] = jnp.where(row8 < PAIR, real, imag)[: 2 * PAIR]

            for turn in range(1, depths):
                remote(send_b.at[target], recv_b.at[layer, me], 1, target, (layer + turn) % depths)

            @pl.when(step < epochs)
            def _():
                remote(send_b.at[target], recv_b.at[layer, me], 1, target, layer)

        local(send_b.at[me], recv_b.at[layer, me], 1)

    owner_part(predict)

    wait_bytes(recv_o, in_sem.at[4])
    inv = 1.0 / jnp.full((8, columns), nv_ref[0], f32)
    seen = jnp.concatenate([recv_o[d, 0:8] for d in range(depths)], axis=1)
    weight = jnp.concatenate([recv_o[d, 8:16] for d in range(depths)], axis=1) * inv
    rowp = lax.broadcasted_iota(jnp.int32, (padded, 8), 0)
    colp = lax.broadcasted_iota(jnp.int32, (padded, 8), 1)
    spread = (rowp // 8 * PAIR + rowp % PAIR == colp).astype(f32)
    seen_wide = jnp.dot(
        spread, seen, precision=lax.Precision.HIGHEST, preferred_element_type=f32
    )
    weight_wide = jnp.dot(
        spread, weight, precision=lax.Precision.HIGHEST, preferred_element_type=f32
    )
    load_i.wait()

    wait_bytes(recv_b, in_sem.at[1])
    for pair in range(pairs):
        for block in range(blocks):
            value = recv_b[0, pair * blocks + block]
            for d in range(1, depths):
                value = value + recv_b[d, pair * blocks + block]
            value = jnp.concatenate([value, value])
            turned = pltpu.roll(value, PAIR, 0)
            rows = slice(pair * 8, pair * 8 + 8)
            wide[rows, block * LANES : (block + 1) * LANES] = jnp.where(
                row8 % 4 < PAIR, value, turned
            )
            wide[rows, half + block * LANES : half + (block + 1) * LANES] = jnp.where(
                row8 % 4 < PAIR, turned, value
            )
    predicted = inverse(wide[...])
    resid = (weight_wide * (predicted - seen_wide)).astype(bf16)
    scatter(forward(resid), send_c)
    to_owners(send_c, recv_c, 2)

    wide[...] = predicted
    mine = pl.ds(pl.multiple_of(layer * width, LANES), width)
    for pair in range(pairs):
        pred_ref[0, pair * PAIR : (pair + 1) * PAIR, :] = wide[pair * 8 : pair * 8 + PAIR, mine]

    def adjoint():
        wait_bytes(recv_c, in_sem.at[2])
        unpack(recv_c)

        @pl.loop(1, epochs + 1)
        def _(step):
            origin = (me + step) % epochs
            real = jnp.zeros((8, LANES), f32)
            imag = jnp.zeros((8, LANES), f32)
            for t in range(epochs):
                at = epochs + t - origin
                a, b, c = lag_abc[at, 0], lag_abc[at, 1], lag_abc[at, 2]
                qr, qi = spec[t, 0], spec[t, 1]
                real = real + (a * qr + b * qi)
                imag = imag + (c * qi - b * qr)
            send_d[origin] = jnp.concatenate([real, imag]).astype(bf16)

            @pl.when(step < epochs)
            def _():
                remote(send_d.at[origin], recv_d.at[me], 3, origin, layer)

        local(send_d.at[me], recv_d.at[me], 3)

    owner_part(adjoint)

    rowc = lax.broadcasted_iota(jnp.int32, (padded, columns), 0) % 8 // PAIR
    prior = jnp.zeros((padded, columns), f32)
    for c in range(channels):
        prior = jnp.where(rowc == c, prior_ref[0, c], prior)
    prior = prior * slip_wide

    wait_bytes(recv_d, in_sem.at[3])
    for pair in range(pairs):
        for block in range(blocks):
            rows = slice(pair * 8, pair * 8 + 8)
            value = recv_d[pair * blocks + block].astype(f32)
            wide[rows, block * LANES : (block + 1) * LANES] = value[0:8]
            wide[rows, half + block * LANES : half + (block + 1) * LANES] = value[8:16]
    held = wide[...].astype(bf16)
    back = jnp.dot(held, i_ref[0], preferred_element_type=f32) + jnp.dot(
        held, i_ref[1], preferred_element_type=f32
    )
    result = -back - prior
    for pair in range(pairs):
        for c in range(channels):
            first = pair * 8 + c * PAIR
            grad_ref[0, 0, c, pair * PAIR : (pair + 1) * PAIR, :] = result[first : first + PAIR]

    sent_to_owners(send_a, 0)
    sent_to_owners(send_c, 2)

    def sent():
        @pl.loop(1, total)
        def _(step):
            wait_bytes(send_b.at[0], out_sem.at[1])

        wait_bytes(send_d.at[pl.ds(0, epochs - 1)], out_sem.at[3])

    owner_part(sent)

    @pl.loop(1, depths)
    def _(step):
        wait_bytes(send_o, out_sem.at[4])


def body(epochs, depths, slip, kernels, lag_index, observed, mask, noise_var, prior_prec):
    columns = slip.shape[-1]
    channels = slip.shape[2]
    kinds = kernels.shape[1]
    rows = slip.shape[3]
    blocks = columns // 2 // LANES
    owners = blocks * rows // PAIR
    padded = rows // PAIR * 8
    forward_table, inverse_table = tables(columns)
    f32, bf16 = jnp.float32, jnp.bfloat16
    vmem = pl.BlockSpec(memory_space=pltpu.VMEM)
    smem = pl.BlockSpec(memory_space=pltpu.SMEM)
    hbm = pl.BlockSpec(memory_space=pltpu.HBM)
    kernels = jnp.swapaxes(kernels, 2, 3)
    return pl.pallas_call(
        functools.partial(kernel, epochs, depths, owners, blocks),
        out_shape=(
            jax.ShapeDtypeStruct(slip.shape, f32),
            jax.ShapeDtypeStruct(observed.shape, f32),
        ),
        in_specs=[smem, smem, smem, hbm, hbm, hbm, hbm, hbm, hbm],
        out_specs=(vmem, vmem),
        scratch_shapes=[
            pltpu.VMEM(slip.shape, bf16),
            pltpu.VMEM(observed.shape, f32),
            pltpu.VMEM(mask.shape, mask.dtype),
            pltpu.VMEM((2, columns, columns), bf16),
            pltpu.VMEM((2, columns, columns), bf16),
            pltpu.VMEM(kernels.shape, f32),
            pltpu.VMEM((owners, 16, LANES), bf16),
            pltpu.VMEM((epochs, 16, LANES), bf16),
            pltpu.VMEM((epochs, 2 * PAIR, LANES), f32),
            pltpu.VMEM((depths, owners, 2 * PAIR, LANES), f32),
            pltpu.VMEM((owners, 16, LANES), bf16),
            pltpu.VMEM((epochs, 16, LANES), bf16),
            pltpu.VMEM((epochs, 16, LANES), bf16),
            pltpu.VMEM((owners, 16, LANES), bf16),
            pltpu.VMEM((16, observed.shape[2]), f32),
            pltpu.VMEM((depths, 16, observed.shape[2]), f32),
            pltpu.VMEM((2, kinds, 8, LANES), f32),
            pltpu.VMEM((kinds, 3, 8, LANES), f32),
            pltpu.VMEM((2 * epochs, 3, 8, LANES), f32),
            pltpu.VMEM((epochs, 2, 8, LANES), f32),
            pltpu.VMEM((padded, columns), f32),
            pltpu.SemaphoreType.DMA((6,)),
            pltpu.SemaphoreType.DMA((5,)),
            pltpu.SemaphoreType.DMA((5,)),
        ],
        compiler_params=pltpu.CompilerParams(
            collective_id=0, has_side_effects=True, vmem_limit_bytes=60 * 1024 * 1024
        ),
    )(
        lag_index, noise_var, prior_prec, slip, observed, mask, kernels,
        jnp.asarray(forward_table), jnp.asarray(inverse_table),
    )


def solution(mesh):
    in_specs = (
        P("epoch", "depth", None, None, None),
        P(None, None, "depth", None, None),
        P(),
        P("epoch", None, "depth"),
        P("epoch", None, "depth"),
        P("epoch"),
        P("depth", None),
    )
    out_specs = (P("epoch", "depth", None, None, None), P("epoch", None, "depth"))
    run = functools.partial(body, mesh.shape["epoch"], mesh.shape["depth"])
    return jax.shard_map(run, mesh=mesh, in_specs=in_specs, out_specs=out_specs, check_vma=False)
```

```python
import functools
import math

import jax
import jax.numpy as jnp
import ml_dtypes
import numpy as np
from jax import lax
from jax.experimental import pallas as pl
from jax.experimental.pallas import tpu as pltpu
from jax.sharding import PartitionSpec as P

LANES = 128
PAIR = 2


def tables(columns):
    half = columns // 2
    x = np.arange(columns, dtype=np.int64)
    angle = 2.0 * math.pi * ((x[:, None] * x[None, :half]) % columns) / columns
    low = np.cos(angle)
    high = -np.sin(angle)
    high[:, 0] = 1.0 - 2.0 * (x % 2)
    forward = np.concatenate([low, high], axis=1)
    scale = np.full((columns,), 2.0 / columns)
    scale[0] = scale[half] = 1.0 / columns
    inverse = (forward * scale[None, :]).T

    def split(table):
        table = table.astype(np.float32)
        top = table.astype(ml_dtypes.bfloat16)
        rest = (table - top.astype(np.float32)).astype(ml_dtypes.bfloat16)
        return np.stack([top, rest])

    return split(forward), split(inverse)


def kernel(
    epochs, depths, owners, blocks,
    lag_ref, nv_ref, prior_ref, slip_hbm, obs_hbm, mask_hbm, k_hbm, f_hbm, i_hbm,
    grad_ref, pred_ref,
    slip_ref, obs_ref, mask_ref, f_ref, i_ref, k_ref, send_a, recv_a, send_b, recv_b, send_c, recv_c, send_d, recv_d,
    send_o, recv_o, mirror, kinds_abc, lag_abc, spec, wide,
    load_sem, out_sem, in_sem,
):
    bf16, f32 = jnp.bfloat16, jnp.float32
    channels = slip_ref.shape[2]
    columns = slip_ref.shape[4]
    half = columns // 2
    kinds = k_ref.shape[1]
    width = obs_ref.shape[2]
    pairs = owners // blocks
    total = epochs * depths
    me = lax.axis_index("epoch")
    layer = lax.axis_index("depth")
    flat = me * depths + layer
    everyone_owns = epochs == owners

    load_f = pltpu.make_async_copy(f_hbm, f_ref, load_sem.at[0])
    load_i = pltpu.make_async_copy(i_hbm, i_ref, load_sem.at[1])
    load_k = pltpu.make_async_copy(k_hbm, k_ref, load_sem.at[2])
    load_s = pltpu.make_async_copy(slip_hbm, slip_ref, load_sem.at[3])
    load_o = pltpu.make_async_copy(obs_hbm, obs_ref, load_sem.at[4])
    load_m = pltpu.make_async_copy(mask_hbm, mask_ref, load_sem.at[5])
    load_k.start()
    load_s.start()
    load_o.start()
    load_m.start()
    load_f.start()
    load_i.start()

    barrier = pltpu.get_barrier_semaphore()

    @pl.loop(1, total)
    def _(step):
        other = (flat + step) % total
        pl.semaphore_signal(
            barrier, inc=1, device_id=(other // depths, other % depths),
            device_id_type=pl.DeviceIdType.MESH,
        )

    def remote(src, dst, number, epoch, depth):
        pltpu.make_async_remote_copy(
            src_ref=src, dst_ref=dst, send_sem=out_sem.at[number], recv_sem=in_sem.at[number],
            device_id=(epoch, depth), device_id_type=pl.DeviceIdType.MESH,
        ).start()

    def local(src, dst, number):
        pltpu.make_async_copy(src, dst, in_sem.at[number]).start()

    def wait_bytes(ref, sem):
        pltpu.make_async_copy(ref, ref, sem).wait()

    def to_owners(send, recv, number, first, some):
        @pl.loop(0, pairs * some)
        def _(step):
            pair = (me // blocks + step // some) % pairs
            owner = pair * blocks + first + (me + step) % some

            @pl.when(owner != me)
            def _():
                remote(send.at[owner], recv.at[me], number, owner, layer)

            @pl.when(owner == me)
            def _():
                local(send.at[owner], recv.at[me], number)

    def sent_to_owners(send, number):
        if everyone_owns:
            wait_bytes(send.at[pl.ds(0, owners - 1)], out_sem.at[number])
        else:
            @pl.when(me < owners)
            def _():
                wait_bytes(send.at[pl.ds(0, owners - 1)], out_sem.at[number])

            @pl.when(me >= owners)
            def _():
                wait_bytes(send, out_sem.at[number])

    def owner_part(part):
        if everyone_owns:
            part()
        else:
            pl.when(me < owners)(part)

    def inverse(value):
        top = value.astype(bf16)
        rest = (value - top.astype(f32)).astype(bf16)
        rows = value.shape[0]
        both = jnp.dot(jnp.concatenate([top, rest]), i_ref[0], preferred_element_type=f32)
        return (both[:rows] + both[rows:]) + jnp.dot(top, i_ref[1], preferred_element_type=f32)

    def forward(field, first, last):
        lanes = slice(first, last)
        return jnp.dot(field, f_ref[0, :, lanes], preferred_element_type=f32) + jnp.dot(
            field, f_ref[1, :, lanes], preferred_element_type=f32
        )

    def transform_out(field, send, recv, number, ready):
        some = PAIR if blocks % PAIR == 0 else 1
        for first in range(0, blocks, some):
            left, right = first * LANES, (first + some) * LANES
            real = forward(field, left, right)
            imag = forward(field, half + left, half + right)
            for pair in range(pairs):
                rows = slice(pair * 8, pair * 8 + 8)
                for k in range(some):
                    lanes = slice(k * LANES, (k + 1) * LANES)
                    send[pair * blocks + first + k] = jnp.concatenate(
                        [real[rows, lanes], imag[rows, lanes]]
                    ).astype(bf16)
            if first == 0:
                ready()
            to_owners(send, recv, number, first, some)

    load_k.wait()

    def prepare():
        block = me % blocks
        row8 = lax.broadcasted_iota(jnp.int32, (8, LANES), 0)
        lane = lax.broadcasted_iota(jnp.int32, (8, LANES), 1)

        def tile(part, kind, place):
            lanes = pl.ds(pl.multiple_of(place * LANES, LANES), LANES)
            out = jnp.zeros((8, LANES), f32)
            for c in range(channels):
                out = jnp.where(row8 // PAIR == c, k_ref[part, kind, c, :, lanes], out)
            return out

        count = 2 * blocks

        @pl.loop(0, kinds)
        def _(kind):
            for part in range(2):
                mirror[part, kind] = tile(part, kind, count - 1 - block)

        j = lax.broadcasted_iota(jnp.int32, (LANES, LANES), 0)
        i = lax.broadcasted_iota(jnp.int32, (LANES, LANES), 1)
        turn = (i + j == LANES).astype(f32)
        turned = jnp.dot(
            mirror[...].reshape(2 * kinds * 8, LANES), turn,
            precision=lax.Precision.HIGHEST, preferred_element_type=f32,
        )
        mirror[...] = turned.reshape(2, kinds, 8, LANES)

        @pl.loop(0, kinds)
        def _(kind):
            first = (count - block) % count
            real = jnp.where(lane == 0, tile(0, kind, first), mirror[0, kind])
            imag = jnp.where(lane == 0, tile(1, kind, first), mirror[1, kind])
            real = 0.5 * (tile(0, kind, block) + real)
            imag = 0.5 * (tile(1, kind, block) - imag)
            middle = tile(0, kind, blocks)
            kinds_abc[kind, 0] = real
            kinds_abc[kind, 1] = imag
            kinds_abc[kind, 2] = jnp.where((lane == 0) & (block == 0), middle, real)

        lag_abc[pl.ds(0, epochs)] = jnp.zeros((epochs, 3, 8, LANES), f32)

        @pl.loop(0, epochs)
        def _(lag):
            lag_abc[epochs + lag] = kinds_abc[lag_ref[lag]]

    owner_part(prepare)

    load_o.wait()
    load_m.wait()
    send_o[0:8] = obs_ref[0]
    send_o[8:16] = mask_ref[0].astype(f32)

    padded = pairs * 8
    row = lax.broadcasted_iota(jnp.int32, (padded, channels * 8), 0)
    source = lax.broadcasted_iota(jnp.int32, (padded, channels * 8), 1)
    wanted = (row % 8) // PAIR * 8 + row // 8 * PAIR + row % PAIR
    order = ((wanted == source) & (row % 8 < channels * PAIR)).astype(bf16)
    load_s.wait()
    slip_rows = jnp.concatenate([slip_ref[0, 0, c].astype(f32) for c in range(channels)])
    slip_wide = jnp.dot(order, slip_rows.astype(bf16), preferred_element_type=f32)

    load_f.wait()
    transform_out(
        slip_wide.astype(bf16), send_a, recv_a, 0,
        lambda: pl.semaphore_wait(barrier, total - 1),
    )

    @pl.loop(1, depths)
    def _(step):
        remote(send_o, recv_o.at[layer], 4, me, (layer + step) % depths)

    local(send_o, recv_o.at[layer], 4)

    def unpack(recv):
        @pl.loop(0, epochs)
        def _(epoch):
            value = recv[epoch].astype(f32)
            spec[epoch, 0] = value[0:8]
            spec[epoch, 1] = value[8:16]

    row8 = lax.broadcasted_iota(jnp.int32, (8, LANES), 0)

    def predict():
        wait_bytes(recv_a, in_sem.at[0])
        unpack(recv_a)

        @pl.loop(1, epochs + 1)
        def _(step):
            target = (me + step) % epochs
            real = jnp.zeros((8, LANES), f32)
            imag = jnp.zeros((8, LANES), f32)
            for s in range(epochs):
                at = epochs + target - s
                a, b, c = lag_abc[at, 0], lag_abc[at, 1], lag_abc[at, 2]
                sr, si = spec[s, 0], spec[s, 1]
                real = real + (a * sr - b * si)
                imag = imag + (c * si + b * sr)
            real = real + pltpu.roll(real, 4, 0)
            real = real + pltpu.roll(real, 2, 0)
            imag = imag + pltpu.roll(imag, 4, 0)
            imag = imag + pltpu.roll(imag, 2, 0)
            send_b[target] = jnp.where(row8 < PAIR, real, imag)[: 2 * PAIR]

            for turn in range(1, depths):
                remote(send_b.at[target], recv_b.at[layer, me], 1, target, (layer + turn) % depths)

            @pl.when(step < epochs)
            def _():
                remote(send_b.at[target], recv_b.at[layer, me], 1, target, layer)

        local(send_b.at[me], recv_b.at[layer, me], 1)

    owner_part(predict)

    wait_bytes(recv_o, in_sem.at[4])
    inv = 1.0 / jnp.full((8, columns), nv_ref[0], f32)
    seen = jnp.concatenate([recv_o[d, 0:8] for d in range(depths)], axis=1)
    weight = jnp.concatenate([recv_o[d, 8:16] for d in range(depths)], axis=1) * inv
    rowp = lax.broadcasted_iota(jnp.int32, (padded, 8), 0)
    colp = lax.broadcasted_iota(jnp.int32, (padded, 8), 1)
    spread = (rowp // 8 * PAIR + rowp % PAIR == colp).astype(f32)
    seen_wide = jnp.dot(
        spread, seen, precision=lax.Precision.HIGHEST, preferred_element_type=f32
    )
    weight_wide = jnp.dot(
        spread, weight, precision=lax.Precision.HIGHEST, preferred_element_type=f32
    )
    load_i.wait()

    wait_bytes(recv_b, in_sem.at[1])
    for pair in range(pairs):
        for block in range(blocks):
            value = recv_b[0, pair * blocks + block]
            for d in range(1, depths):
                value = value + recv_b[d, pair * blocks + block]
            value = jnp.concatenate([value, value])
            turned = pltpu.roll(value, PAIR, 0)
            rows = slice(pair * 8, pair * 8 + 8)
            wide[rows, block * LANES : (block + 1) * LANES] = jnp.where(
                row8 % 4 < PAIR, value, turned
            )
            wide[rows, half + block * LANES : half + (block + 1) * LANES] = jnp.where(
                row8 % 4 < PAIR, turned, value
            )
    predicted = inverse(wide[...])
    resid = (weight_wide * (predicted - seen_wide)).astype(bf16)
    transform_out(resid, send_c, recv_c, 2, lambda: None)

    wide[...] = predicted
    mine = pl.ds(pl.multiple_of(layer * width, LANES), width)
    for pair in range(pairs):
        pred_ref[0, pair * PAIR : (pair + 1) * PAIR, :] = wide[pair * 8 : pair * 8 + PAIR, mine]

    def adjoint():
        wait_bytes(recv_c, in_sem.at[2])
        unpack(recv_c)

        @pl.loop(1, epochs + 1)
        def _(step):
            origin = (me + step) % epochs
            real = jnp.zeros((8, LANES), f32)
            imag = jnp.zeros((8, LANES), f32)
            for t in range(epochs):
                at = epochs + t - origin
                a, b, c = lag_abc[at, 0], lag_abc[at, 1], lag_abc[at, 2]
                qr, qi = spec[t, 0], spec[t, 1]
                real = real + (a * qr + b * qi)
                imag = imag + (c * qi - b * qr)
            send_d[origin] = jnp.concatenate([real, imag]).astype(bf16)

            @pl.when(step < epochs)
            def _():
                remote(send_d.at[origin], recv_d.at[me], 3, origin, layer)

        local(send_d.at[me], recv_d.at[me], 3)

    owner_part(adjoint)

    rowc = lax.broadcasted_iota(jnp.int32, (padded, columns), 0) % 8 // PAIR
    prior = jnp.zeros((padded, columns), f32)
    for c in range(channels):
        prior = jnp.where(rowc == c, prior_ref[0, c], prior)
    prior = prior * slip_wide

    wait_bytes(recv_d, in_sem.at[3])
    for pair in range(pairs):
        for block in range(blocks):
            rows = slice(pair * 8, pair * 8 + 8)
            value = recv_d[pair * blocks + block].astype(f32)
            wide[rows, block * LANES : (block + 1) * LANES] = value[0:8]
            wide[rows, half + block * LANES : half + (block + 1) * LANES] = value[8:16]
    held = wide[...].astype(bf16)
    back = jnp.dot(held, i_ref[0], preferred_element_type=f32) + jnp.dot(
        held, i_ref[1], preferred_element_type=f32
    )
    result = -back - prior
    for pair in range(pairs):
        for c in range(channels):
            first = pair * 8 + c * PAIR
            grad_ref[0, 0, c, pair * PAIR : (pair + 1) * PAIR, :] = result[first : first + PAIR]

    sent_to_owners(send_a, 0)
    sent_to_owners(send_c, 2)

    def sent():
        @pl.loop(1, total)
        def _(step):
            wait_bytes(send_b.at[0], out_sem.at[1])

        wait_bytes(send_d.at[pl.ds(0, epochs - 1)], out_sem.at[3])

    owner_part(sent)

    @pl.loop(1, depths)
    def _(step):
        wait_bytes(send_o, out_sem.at[4])


def hand_over(grad_in, pred_in, grad_out, pred_out, sem):
    channels = grad_in.shape[2]
    copies = [
        pltpu.make_async_copy(grad_in.at[0, 0, c], grad_out.at[0, 0, c], sem.at[c])
        for c in range(channels)
    ]
    copies.append(pltpu.make_async_copy(pred_in, pred_out, sem.at[channels]))
    for copy in copies:
        copy.start()
    for copy in copies:
        copy.wait()


def body(epochs, depths, slip, kernels, lag_index, observed, mask, noise_var, prior_prec):
    columns = slip.shape[-1]
    channels = slip.shape[2]
    kinds = kernels.shape[1]
    rows = slip.shape[3]
    blocks = columns // 2 // LANES
    owners = blocks * rows // PAIR
    padded = rows // PAIR * 8
    forward_table, inverse_table = tables(columns)
    f32, bf16 = jnp.float32, jnp.bfloat16
    vmem = pl.BlockSpec(memory_space=pltpu.VMEM)
    smem = pl.BlockSpec(memory_space=pltpu.SMEM)
    hbm = pl.BlockSpec(memory_space=pltpu.HBM)
    kernels = jnp.swapaxes(kernels, 2, 3)
    shapes = (
        jax.ShapeDtypeStruct(slip.shape, f32),
        jax.ShapeDtypeStruct(observed.shape, f32),
    )
    results = pl.pallas_call(
        functools.partial(kernel, epochs, depths, owners, blocks),
        out_shape=shapes,
        in_specs=[smem, smem, smem, hbm, hbm, hbm, hbm, hbm, hbm],
        out_specs=(vmem, vmem),
        scratch_shapes=[
            pltpu.VMEM(slip.shape, bf16),
            pltpu.VMEM(observed.shape, f32),
            pltpu.VMEM(mask.shape, mask.dtype),
            pltpu.VMEM((2, columns, columns), bf16),
            pltpu.VMEM((2, columns, columns), bf16),
            pltpu.VMEM(kernels.shape, f32),
            pltpu.VMEM((owners, 16, LANES), bf16),
            pltpu.VMEM((epochs, 16, LANES), bf16),
            pltpu.VMEM((epochs, 2 * PAIR, LANES), f32),
            pltpu.VMEM((depths, owners, 2 * PAIR, LANES), f32),
            pltpu.VMEM((owners, 16, LANES), bf16),
            pltpu.VMEM((epochs, 16, LANES), bf16),
            pltpu.VMEM((epochs, 16, LANES), bf16),
            pltpu.VMEM((owners, 16, LANES), bf16),
            pltpu.VMEM((16, observed.shape[2]), f32),
            pltpu.VMEM((depths, 16, observed.shape[2]), f32),
            pltpu.VMEM((2, kinds, 8, LANES), f32),
            pltpu.VMEM((kinds, 3, 8, LANES), f32),
            pltpu.VMEM((2 * epochs, 3, 8, LANES), f32),
            pltpu.VMEM((epochs, 2, 8, LANES), f32),
            pltpu.VMEM((padded, columns), f32),
            pltpu.SemaphoreType.DMA((6,)),
            pltpu.SemaphoreType.DMA((5,)),
            pltpu.SemaphoreType.DMA((5,)),
        ],
        compiler_params=pltpu.CompilerParams(
            collective_id=0, has_side_effects=True, vmem_limit_bytes=60 * 1024 * 1024
        ),
    )(
        lag_index, noise_var, prior_prec, slip, observed, mask, kernels,
        jnp.asarray(forward_table), jnp.asarray(inverse_table),
    )
    return pl.pallas_call(
        hand_over,
        out_shape=shapes,
        in_specs=[hbm, hbm],
        out_specs=(hbm, hbm),
        scratch_shapes=[pltpu.SemaphoreType.DMA((channels + 1,))],
    )(*results)


def solution(mesh):
    in_specs = (
        P("epoch", "depth", None, None, None),
        P(None, None, "depth", None, None),
        P(),
        P("epoch", None, "depth"),
        P("epoch", None, "depth"),
        P("epoch"),
        P("depth", None),
    )
    out_specs = (P("epoch", "depth", None, None, None), P("epoch", None, "depth"))
    run = functools.partial(body, mesh.shape["epoch"], mesh.shape["depth"])
    return jax.shard_map(run, mesh=mesh, in_specs=in_specs, out_specs=out_specs, check_vma=False)
```

```python
import functools
import math

import jax
import jax.numpy as jnp
import ml_dtypes
import numpy as np
from jax import lax
from jax.experimental import pallas as pl
from jax.experimental.pallas import tpu as pltpu
from jax.sharding import PartitionSpec as P

LANES = 128
PAIR = 2


def tables(columns):
    half = columns // 2
    x = np.arange(columns, dtype=np.int64)
    angle = 2.0 * math.pi * ((x[:, None] * x[None, :half]) % columns) / columns
    low = np.cos(angle)
    high = -np.sin(angle)
    high[:, 0] = 1.0 - 2.0 * (x % 2)
    forward = np.concatenate([low, high], axis=1)
    scale = np.full((columns,), 2.0 / columns)
    scale[0] = scale[half] = 1.0 / columns
    inverse = (forward * scale[None, :]).T

    def split(table):
        table = table.astype(np.float32)
        top = table.astype(ml_dtypes.bfloat16)
        rest = (table - top.astype(np.float32)).astype(ml_dtypes.bfloat16)
        return np.stack([top, rest])

    return split(forward), split(inverse)


def kernel(
    epochs, depths, owners, blocks,
    lag_ref, nv_ref, prior_ref, slip_hbm, obs_hbm, mask_hbm, k_hbm, f_hbm, i_hbm,
    grad_ref, pred_ref,
    slip_ref, obs_ref, mask_ref, f_ref, i_ref, k_ref, send_a, recv_a, send_b, recv_b, send_c, recv_c, send_d, recv_d,
    send_o, recv_o, mirror, kinds_abc, lag_abc, spec, wide,
    load_sem, out_sem, in_sem,
):
    bf16, f32 = jnp.bfloat16, jnp.float32
    channels = slip_ref.shape[2]
    columns = slip_ref.shape[4]
    half = columns // 2
    kinds = k_ref.shape[1]
    width = obs_ref.shape[2]
    pairs = owners // blocks
    total = epochs * depths
    me = lax.axis_index("epoch")
    layer = lax.axis_index("depth")
    flat = me * depths + layer
    everyone_owns = epochs == owners

    load_f = pltpu.make_async_copy(f_hbm, f_ref, load_sem.at[0])
    load_i = pltpu.make_async_copy(i_hbm, i_ref, load_sem.at[1])
    load_k = pltpu.make_async_copy(k_hbm, k_ref, load_sem.at[2])
    load_s = pltpu.make_async_copy(slip_hbm, slip_ref, load_sem.at[3])
    load_o = pltpu.make_async_copy(obs_hbm, obs_ref, load_sem.at[4])
    load_m = pltpu.make_async_copy(mask_hbm, mask_ref, load_sem.at[5])
    load_k.start()
    load_s.start()
    load_o.start()
    load_m.start()
    load_f.start()
    load_i.start()

    barrier = pltpu.get_barrier_semaphore()

    @pl.loop(1, total)
    def _(step):
        other = (flat + step) % total
        pl.semaphore_signal(
            barrier, inc=1, device_id=(other // depths, other % depths),
            device_id_type=pl.DeviceIdType.MESH,
        )

    def remote(src, dst, number, epoch, depth):
        pltpu.make_async_remote_copy(
            src_ref=src, dst_ref=dst, send_sem=out_sem.at[number], recv_sem=in_sem.at[number],
            device_id=(epoch, depth), device_id_type=pl.DeviceIdType.MESH,
        ).start()

    def local(src, dst, number):
        pltpu.make_async_copy(src, dst, in_sem.at[number]).start()

    def wait_bytes(ref, sem):
        pltpu.make_async_copy(ref, ref, sem).wait()

    def to_owners(send, recv, number, first, some):
        @pl.loop(0, pairs * some)
        def _(step):
            pair = (me // blocks + step // some) % pairs
            owner = pair * blocks + first + (me + step) % some

            @pl.when(owner != me)
            def _():
                remote(send.at[owner], recv.at[me], number, owner, layer)

            @pl.when(owner == me)
            def _():
                local(send.at[owner], recv.at[me], number)

    def sent_to_owners(send, number):
        if everyone_owns:
            wait_bytes(send.at[pl.ds(0, owners - 1)], out_sem.at[number])
        else:
            @pl.when(me < owners)
            def _():
                wait_bytes(send.at[pl.ds(0, owners - 1)], out_sem.at[number])

            @pl.when(me >= owners)
            def _():
                wait_bytes(send, out_sem.at[number])

    def owner_part(part):
        if everyone_owns:
            part()
        else:
            pl.when(me < owners)(part)

    def inverse(value):
        top = value.astype(bf16)
        rest = (value - top.astype(f32)).astype(bf16)
        rows = value.shape[0]
        both = jnp.dot(jnp.concatenate([top, rest]), i_ref[0], preferred_element_type=f32)
        return (both[:rows] + both[rows:]) + jnp.dot(top, i_ref[1], preferred_element_type=f32)

    def forward(field, first, last):
        lanes = slice(first, last)
        return jnp.dot(field, f_ref[0, :, lanes], preferred_element_type=f32) + jnp.dot(
            field, f_ref[1, :, lanes], preferred_element_type=f32
        )

    def transform_out(field, send, recv, number, ready):
        some = PAIR if blocks % PAIR == 0 else 1
        for first in range(0, blocks, some):
            left, right = first * LANES, (first + some) * LANES
            real = forward(field, left, right)
            imag = forward(field, half + left, half + right)
            for pair in range(pairs):
                rows = slice(pair * 8, pair * 8 + 8)
                for k in range(some):
                    lanes = slice(k * LANES, (k + 1) * LANES)
                    send[pair * blocks + first + k] = jnp.concatenate(
                        [real[rows, lanes], imag[rows, lanes]]
                    ).astype(bf16)
            if first == 0:
                ready()
            to_owners(send, recv, number, first, some)

    load_k.wait()

    def prepare():
        block = me % blocks
        row8 = lax.broadcasted_iota(jnp.int32, (8, LANES), 0)
        lane = lax.broadcasted_iota(jnp.int32, (8, LANES), 1)

        def tile(part, kind, place):
            lanes = pl.ds(pl.multiple_of(place * LANES, LANES), LANES)
            out = jnp.zeros((8, LANES), f32)
            for c in range(channels):
                out = jnp.where(row8 // PAIR == c, k_ref[part, kind, c, :, lanes], out)
            return out

        count = 2 * blocks

        @pl.loop(0, kinds)
        def _(kind):
            for part in range(2):
                mirror[part, kind] = tile(part, kind, count - 1 - block)

        j = lax.broadcasted_iota(jnp.int32, (LANES, LANES), 0)
        i = lax.broadcasted_iota(jnp.int32, (LANES, LANES), 1)
        turn = (i + j == LANES).astype(f32)
        turned = jnp.dot(
            mirror[...].reshape(2 * kinds * 8, LANES), turn,
            precision=lax.Precision.HIGHEST, preferred_element_type=f32,
        )
        mirror[...] = turned.reshape(2, kinds, 8, LANES)

        @pl.loop(0, kinds)
        def _(kind):
            first = (count - block) % count
            real = jnp.where(lane == 0, tile(0, kind, first), mirror[0, kind])
            imag = jnp.where(lane == 0, tile(1, kind, first), mirror[1, kind])
            real = 0.5 * (tile(0, kind, block) + real)
            imag = 0.5 * (tile(1, kind, block) - imag)
            middle = tile(0, kind, blocks)
            kinds_abc[kind, 0] = real
            kinds_abc[kind, 1] = imag
            kinds_abc[kind, 2] = jnp.where((lane == 0) & (block == 0), middle, real)

        lag_abc[pl.ds(0, epochs)] = jnp.zeros((epochs, 3, 8, LANES), f32)

        @pl.loop(0, epochs)
        def _(lag):
            lag_abc[epochs + lag] = kinds_abc[lag_ref[lag]]

    owner_part(prepare)

    load_o.wait()
    load_m.wait()
    send_o[0:8] = obs_ref[0]
    send_o[8:16] = mask_ref[0].astype(f32)

    padded = pairs * 8
    row = lax.broadcasted_iota(jnp.int32, (padded, channels * 8), 0)
    source = lax.broadcasted_iota(jnp.int32, (padded, channels * 8), 1)
    wanted = (row % 8) // PAIR * 8 + row // 8 * PAIR + row % PAIR
    order = ((wanted == source) & (row % 8 < channels * PAIR)).astype(bf16)
    load_s.wait()
    slip_rows = jnp.concatenate([slip_ref[0, 0, c].astype(f32) for c in range(channels)])
    slip_wide = jnp.dot(order, slip_rows.astype(bf16), preferred_element_type=f32)

    load_f.wait()
    transform_out(
        slip_wide.astype(bf16), send_a, recv_a, 0,
        lambda: pl.semaphore_wait(barrier, total - 1),
    )

    @pl.loop(1, depths)
    def _(step):
        remote(send_o, recv_o.at[layer], 4, me, (layer + step) % depths)

    local(send_o, recv_o.at[layer], 4)

    def unpack(recv):
        @pl.loop(0, epochs)
        def _(epoch):
            value = recv[epoch].astype(f32)
            spec[epoch, 0] = value[0:8]
            spec[epoch, 1] = value[8:16]

    row8 = lax.broadcasted_iota(jnp.int32, (8, LANES), 0)

    def predict():
        wait_bytes(recv_a, in_sem.at[0])
        unpack(recv_a)

        @pl.loop(1, epochs + 1)
        def _(step):
            target = (me + step) % epochs
            real = jnp.zeros((8, LANES), f32)
            imag = jnp.zeros((8, LANES), f32)
            for s in range(epochs):
                at = epochs + target - s
                a, b, c = lag_abc[at, 0], lag_abc[at, 1], lag_abc[at, 2]
                sr, si = spec[s, 0], spec[s, 1]
                real = real + (a * sr - b * si)
                imag = imag + (c * si + b * sr)
            real = real + pltpu.roll(real, 4, 0)
            real = real + pltpu.roll(real, 2, 0)
            imag = imag + pltpu.roll(imag, 4, 0)
            imag = imag + pltpu.roll(imag, 2, 0)
            send_b[target] = jnp.where(row8 < PAIR, real, imag)[: 2 * PAIR]

            for turn in range(1, depths):
                remote(send_b.at[target], recv_b.at[layer, me], 1, target, (layer + turn) % depths)

            @pl.when(step < epochs)
            def _():
                remote(send_b.at[target], recv_b.at[layer, me], 1, target, layer)

        local(send_b.at[me], recv_b.at[layer, me], 1)

    owner_part(predict)

    wait_bytes(recv_o, in_sem.at[4])
    inv = 1.0 / jnp.full((8, columns), nv_ref[0], f32)
    seen = jnp.concatenate([recv_o[d, 0:8] for d in range(depths)], axis=1)
    weight = jnp.concatenate([recv_o[d, 8:16] for d in range(depths)], axis=1) * inv
    rowp = lax.broadcasted_iota(jnp.int32, (padded, 8), 0)
    colp = lax.broadcasted_iota(jnp.int32, (padded, 8), 1)
    spread = (rowp // 8 * PAIR + rowp % PAIR == colp).astype(f32)
    seen_wide = jnp.dot(
        spread, seen, precision=lax.Precision.HIGHEST, preferred_element_type=f32
    )
    weight_wide = jnp.dot(
        spread, weight, precision=lax.Precision.HIGHEST, preferred_element_type=f32
    )
    load_i.wait()

    wait_bytes(recv_b, in_sem.at[1])
    for pair in range(pairs):
        for block in range(blocks):
            value = recv_b[0, pair * blocks + block]
            for d in range(1, depths):
                value = value + recv_b[d, pair * blocks + block]
            value = jnp.concatenate([value, value])
            turned = pltpu.roll(value, PAIR, 0)
            rows = slice(pair * 8, pair * 8 + 8)
            wide[rows, block * LANES : (block + 1) * LANES] = jnp.where(
                row8 % 4 < PAIR, value, turned
            )
            wide[rows, half + block * LANES : half + (block + 1) * LANES] = jnp.where(
                row8 % 4 < PAIR, turned, value
            )
    predicted = inverse(wide[...])
    resid = (weight_wide * (predicted - seen_wide)).astype(bf16)
    transform_out(resid, send_c, recv_c, 2, lambda: None)

    wide[...] = predicted
    mine = pl.ds(pl.multiple_of(layer * width, LANES), width)
    for pair in range(pairs):
        pred_ref[0, pair * PAIR : (pair + 1) * PAIR, :] = wide[pair * 8 : pair * 8 + PAIR, mine]

    def adjoint():
        wait_bytes(recv_c, in_sem.at[2])
        unpack(recv_c)

        @pl.loop(1, epochs + 1)
        def _(step):
            origin = (me + step) % epochs
            real = jnp.zeros((8, LANES), f32)
            imag = jnp.zeros((8, LANES), f32)
            for t in range(epochs):
                at = epochs + t - origin
                a, b, c = lag_abc[at, 0], lag_abc[at, 1], lag_abc[at, 2]
                qr, qi = spec[t, 0], spec[t, 1]
                real = real + (a * qr + b * qi)
                imag = imag + (c * qi - b * qr)
            send_d[origin] = jnp.concatenate([real, imag]).astype(bf16)

            @pl.when(step < epochs)
            def _():
                remote(send_d.at[origin], recv_d.at[me], 3, origin, layer)

        local(send_d.at[me], recv_d.at[me], 3)

    owner_part(adjoint)

    rowc = lax.broadcasted_iota(jnp.int32, (padded, columns), 0) % 8 // PAIR
    prior = jnp.zeros((padded, columns), f32)
    for c in range(channels):
        prior = jnp.where(rowc == c, prior_ref[0, c], prior)
    prior = prior * slip_wide

    wait_bytes(recv_d, in_sem.at[3])
    for pair in range(pairs):
        for block in range(blocks):
            rows = slice(pair * 8, pair * 8 + 8)
            value = recv_d[pair * blocks + block].astype(f32)
            wide[rows, block * LANES : (block + 1) * LANES] = value[0:8]
            wide[rows, half + block * LANES : half + (block + 1) * LANES] = value[8:16]
    held = wide[...].astype(bf16)
    back = jnp.dot(held, i_ref[0], preferred_element_type=f32) + jnp.dot(
        held, i_ref[1], preferred_element_type=f32
    )
    result = -back - prior
    for pair in range(pairs):
        for c in range(channels):
            first = pair * 8 + c * PAIR
            grad_ref[0, 0, c, pair * PAIR : (pair + 1) * PAIR, :] = result[first : first + PAIR]

    sent_to_owners(send_a, 0)
    sent_to_owners(send_c, 2)

    def sent():
        @pl.loop(1, total)
        def _(step):
            wait_bytes(send_b.at[0], out_sem.at[1])

        wait_bytes(send_d.at[pl.ds(0, epochs - 1)], out_sem.at[3])

    owner_part(sent)

    @pl.loop(1, depths)
    def _(step):
        wait_bytes(send_o, out_sem.at[4])


def hand_over(grad_in, pred_in, grad_out, pred_out):
    grad_out[...] = grad_in[...]
    pred_out[...] = pred_in[...]


def body(epochs, depths, slip, kernels, lag_index, observed, mask, noise_var, prior_prec):
    columns = slip.shape[-1]
    channels = slip.shape[2]
    kinds = kernels.shape[1]
    rows = slip.shape[3]
    blocks = columns // 2 // LANES
    owners = blocks * rows // PAIR
    padded = rows // PAIR * 8
    forward_table, inverse_table = tables(columns)
    f32, bf16 = jnp.float32, jnp.bfloat16
    vmem = pl.BlockSpec(memory_space=pltpu.VMEM)
    smem = pl.BlockSpec(memory_space=pltpu.SMEM)
    hbm = pl.BlockSpec(memory_space=pltpu.HBM)
    kernels = jnp.swapaxes(kernels, 2, 3)
    shapes = (
        jax.ShapeDtypeStruct(slip.shape, f32),
        jax.ShapeDtypeStruct(observed.shape, f32),
    )
    results = pl.pallas_call(
        functools.partial(kernel, epochs, depths, owners, blocks),
        out_shape=shapes,
        in_specs=[smem, smem, smem, hbm, hbm, hbm, hbm, hbm, hbm],
        out_specs=(vmem, vmem),
        scratch_shapes=[
            pltpu.VMEM(slip.shape, bf16),
            pltpu.VMEM(observed.shape, f32),
            pltpu.VMEM(mask.shape, mask.dtype),
            pltpu.VMEM((2, columns, columns), bf16),
            pltpu.VMEM((2, columns, columns), bf16),
            pltpu.VMEM(kernels.shape, f32),
            pltpu.VMEM((owners, 16, LANES), bf16),
            pltpu.VMEM((epochs, 16, LANES), bf16),
            pltpu.VMEM((epochs, 2 * PAIR, LANES), f32),
            pltpu.VMEM((depths, owners, 2 * PAIR, LANES), f32),
            pltpu.VMEM((owners, 16, LANES), bf16),
            pltpu.VMEM((epochs, 16, LANES), bf16),
            pltpu.VMEM((epochs, 16, LANES), bf16),
            pltpu.VMEM((owners, 16, LANES), bf16),
            pltpu.VMEM((16, observed.shape[2]), f32),
            pltpu.VMEM((depths, 16, observed.shape[2]), f32),
            pltpu.VMEM((2, kinds, 8, LANES), f32),
            pltpu.VMEM((kinds, 3, 8, LANES), f32),
            pltpu.VMEM((2 * epochs, 3, 8, LANES), f32),
            pltpu.VMEM((epochs, 2, 8, LANES), f32),
            pltpu.VMEM((padded, columns), f32),
            pltpu.SemaphoreType.DMA((6,)),
            pltpu.SemaphoreType.DMA((5,)),
            pltpu.SemaphoreType.DMA((5,)),
        ],
        compiler_params=pltpu.CompilerParams(
            collective_id=0, has_side_effects=True, vmem_limit_bytes=60 * 1024 * 1024
        ),
    )(
        lag_index, noise_var, prior_prec, slip, observed, mask, kernels,
        jnp.asarray(forward_table), jnp.asarray(inverse_table),
    )
    return pl.pallas_call(
        hand_over,
        out_shape=shapes,
        in_specs=[vmem, vmem],
        out_specs=(vmem, vmem),
    )(*results)


def solution(mesh):
    in_specs = (
        P("epoch", "depth", None, None, None),
        P(None, None, "depth", None, None),
        P(),
        P("epoch", None, "depth"),
        P("epoch", None, "depth"),
        P("epoch"),
        P("depth", None),
    )
    out_specs = (P("epoch", "depth", None, None, None), P("epoch", None, "depth"))
    run = functools.partial(body, mesh.shape["epoch"], mesh.shape["depth"])
    return jax.shard_map(run, mesh=mesh, in_specs=in_specs, out_specs=out_specs, check_vma=False)
```
